32 devices in a mesh: section: 4 (over y, x), trial: 8 (over z, core).
Axes of the slice: x: 2, y: 2, z: 4, core: 2. Of those that a mesh axis runs over, the one named last changes fastest.
Arguments:
- spike_rates: bfloat16 [512, 16, 256], P(None, 'trial'), may hold values from -6 to 6
- first_preactivation: bfloat16 [1024, 16, 256], P('section', 'trial'), may hold values from -6 to 6
- second_preactivation: bfloat16 [1024, 16, 256], P('section', 'trial'), may hold values from -6 to 6
- output_gradient: bfloat16 [1024, 16, 256], P('section', 'trial'), may hold values from -0.29882812 to 0.29882812
- first_kernel: bfloat16 [3, 1024, 1024], P(None, None, 'section'), may hold values from -0.109375 to 0.109375
- second_kernel: bfloat16 [3, 1024, 1024], P(None, None, 'section'), may hold values from -0.109375 to 0.109375
- session_of: int32 [16], P('trial'), may hold values from 0 to 7, never falling along the last dimension, each value on 1 to 6 neighbouring positions
Outputs:
- readin_grad: bfloat16 [8, 512, 1024], P(None, 'trial', 'section')
The draws below stay inside these ranges and needn't reach their ends.
Inputs may be any that keep to these rules, and one draw needn't show every extreme that they name: `session_of`: the trials of a session are consecutive; every session has 1 to 6 trials, and one has exactly 6.
All inputs are finite; a program needn't handle non-finite values.
Results may differ from the reference program's by a relative error of at most 0.017.
Values may be sent and summed in bfloat16 or wider, within the bound.
A program may use at most 64 MiB of HBM per device.

```python
import math
import jax
import jax.numpy as jnp
import numpy as np
from jax import lax

C = 1024
NEUR = 512
L = 256
FIRST_DILATION = 32
SECOND_DILATION = 64
TRIALS = 16
SESSIONS = 8
MOST = 6


def levels(own_key, extent, split, smallest, high):
    factor_of, own = 1.0, jax.random.fold_in(own_key, 6)
    for dim, blocks in split:
        draws = jnp.exp(jax.random.uniform(jax.random.fold_in(own, dim), (blocks,), jnp.float32, smallest / len(split), high / len(split)))
        factor_of = factor_of * jnp.repeat(draws, extent[dim] // blocks).reshape([-1 if axis == dim else 1 for axis in range(len(extent))])
    return factor_of


def length_profile(number_of, total, bound, slope):
    loads = [(1 << 20) // math.isqrt(grade ** slope) + 1 for grade in range(2, number_of + 1)]
    rest, holding = total - bound - (number_of - 1), [1] * (number_of - 1)
    while rest > 0:
        candidates = [i for i in range(number_of - 1) if holding[i] < bound]
        mass, left = sum([loads[i] for i in candidates]), rest
        for i in candidates:
            addition = min(bound - holding[i], max(1, left * loads[i] // mass), rest)
            holding[i] = holding[i] + addition
            rest = rest - addition
    return np.array([bound] + holding)


def uneven_parts(own_key, amount, total, reach, slope):
    if amount == 2:
        one = jax.random.randint(own_key, (), max(1, total - reach), min(reach, total - 1) + 1)
        return jnp.stack([one, total - one])
    tallies = jnp.asarray(length_profile(amount, total, reach, slope), jnp.int32)
    couples = (amount - 1) // 2
    source_of, taker = tallies[1:1 + 2 * couples:2], tallies[2:2 + 2 * couples:2]
    room = jnp.minimum(source_of - 1, reach - taker)
    moved = jax.random.randint(jax.random.fold_in(own_key, 1), (couples,), 0, 1 << 20) % (room + 1)
    tallies = tallies.at[1:1 + 2 * couples:2].set(source_of - moved).at[2:2 + 2 * couples:2].set(taker + moved)
    return tallies[jax.random.permutation(jax.random.fold_in(own_key, 2), amount)]


def scatter_about(rng, shape, width, bound, pieces=(), kind=jnp.bfloat16):
    drawn = width * jax.random.normal(rng, shape, jnp.float32)
    if pieces:
        drawn = drawn * levels(rng, shape, pieces, -0.22, 0.18)
    return jnp.clip(drawn, -bound, bound).astype(kind)


def setup_inputs(seed: int = 0) -> dict:
    keys = jax.random.split(jax.random.key(seed), 8)
    spike_rates = scatter_about(keys[0], (NEUR, TRIALS, L), 1.0, 6.0, ((1, 8),))
    first_preactivation = scatter_about(keys[1], (C, TRIALS, L), 1.0, 6.0, ((0, 4), (1, 8)))
    second_preactivation = scatter_about(keys[2], (C, TRIALS, L), 1.0, 6.0, ((0, 4), (1, 8)))
    output_gradient = scatter_about(keys[3], (C, TRIALS, L), 0.05, 0.29882812, ((0, 4), (1, 8)))
    first_kernel = scatter_about(keys[4], (3, C, C), (3 * C) ** -0.5, 0.109375, ((2, 4),))
    second_kernel = scatter_about(keys[5], (3, C, C), (3 * C) ** -0.5, 0.109375, ((2, 4),))
    session_of = jnp.searchsorted(jnp.cumsum(uneven_parts(keys[6], SESSIONS, TRIALS, MOST, 2)), jnp.arange(TRIALS), side="right").astype(jnp.int32)
    return {"spike_rates": spike_rates, "first_preactivation": first_preactivation, "second_preactivation": second_preactivation, "output_gradient": output_gradient, "first_kernel": first_kernel, "second_kernel": second_kernel, "session_of": session_of}


def gelu_slope(preact):
    values = preact.astype(jnp.float32)
    normal_cdf = 0.5 * (1.0 + lax.erf(values * (1.0 / math.sqrt(2.0))))
    density = jnp.exp(-0.5 * values * values) * (1.0 / math.sqrt(2.0 * math.pi))
    return normal_cdf + values * density

def shift_ahead(values, offset):
    padding = [(0, 0)] * (values.ndim - 1) + [(0, offset)]
    return jnp.pad(values[..., offset:], padding)

def conv_back(weights, flow_grad, spacing):
    flow_wide = flow_grad.astype(jnp.float32)
    running = None
    for kernel_tap in range(3):
        term_tap = jnp.einsum('co,oil->cil', weights[kernel_tap].astype(jnp.float32), flow_wide, precision=lax.Precision.HIGHEST)
        if kernel_tap > 0:
            term_tap = shift_ahead(term_tap, kernel_tap * spacing)
        running = term_tap if running is None else running + term_tap
    return running

def layer_backprop(upstream, preact, weights, spacing):
    flow_grad = (upstream.astype(jnp.float32) * gelu_slope(preact)).astype(jnp.bfloat16)
    return (upstream.astype(jnp.float32) + conv_back(weights, flow_grad, spacing)).astype(jnp.bfloat16)

def reference(spike_rates, first_preactivation, second_preactivation, output_gradient, first_kernel, second_kernel, session_of):
    upstream_gradient = layer_backprop(output_gradient, second_preactivation, second_kernel, SECOND_DILATION)
    input_gradient = layer_backprop(upstream_gradient, first_preactivation, first_kernel, FIRST_DILATION)

    def add_trial(carry, index):
        sample = lax.dynamic_slice_in_dim(spike_rates, index, 1, 1)[:, 0, :].astype(jnp.float32)
        grad_trial = lax.dynamic_slice_in_dim(input_gradient, index, 1, 1)[:, 0, :].astype(jnp.float32)
        product = jnp.dot(sample, grad_trial.T, precision=lax.Precision.HIGHEST)
        owner = lax.dynamic_slice_in_dim(session_of, index, 1, 0)[0].astype(jnp.int32)
        current = lax.dynamic_slice_in_dim(carry, owner, 1, 0)
        carry = lax.dynamic_update_slice_in_dim(carry, current + product[None], owner, 0)
        return (carry, None)
    start_sums = jnp.zeros((SESSIONS, NEUR, C), jnp.float32)
    result, _ = lax.scan(add_trial, start_sums, jnp.arange(TRIALS, dtype=jnp.int32))
    return result.astype(jnp.bfloat16)
```

```python
import functools
import math

import jax
import jax.numpy as jnp
from jax import lax
from jax.experimental import pallas as pl
from jax.experimental.pallas import tpu as pltpu
from jax.sharding import PartitionSpec as P

FIRST_DILATION = 32
SECOND_DILATION = 64
MOST = 6


def gelu_slope(preact):
    values = preact.astype(jnp.float32)
    normal_cdf = 0.5 * (1.0 + lax.erf(values * (1.0 / math.sqrt(2.0))))
    density = jnp.exp(-0.5 * values * values) * (1.0 / math.sqrt(2.0 * math.pi))
    return normal_cdf + values * density


def shift_ahead(values, offset):
    padding = [(0, 0)] * (values.ndim - 1) + [(0, offset)]
    return jnp.pad(values[..., offset:], padding)


def tap_sum(weights, flow_grad, spacing):
    running = None
    for kernel_tap in range(3):
        term_tap = lax.dot_general(
            weights[kernel_tap],
            flow_grad,
            (((1,), (0,)), ((), ())),
            preferred_element_type=jnp.float32,
        )
        if kernel_tap > 0:
            term_tap = shift_ahead(term_tap, kernel_tap * spacing)
        running = term_tap if running is None else running + term_tap
    return running


def layer_backprop(upstream, preact, turned, spacing):
    flow_grad = (upstream.astype(jnp.float32) * gelu_slope(preact)).astype(jnp.bfloat16)
    back_sum = tap_sum(turned, lax.all_gather(flow_grad, "section", axis=0, tiled=True), spacing)
    return (upstream.astype(jnp.float32) + back_sum).astype(jnp.bfloat16)


def body(
    spike_rates,
    first_preactivation,
    second_preactivation,
    output_gradient,
    first_kernel,
    second_kernel,
    session_of,
):
    first_flipped_kernel, second_flipped_kernel = (
        lax.all_to_all(first_kernel, "section", split_axis=1, concat_axis=2, tiled=True),
        lax.all_to_all(second_kernel, "section", split_axis=1, concat_axis=2, tiled=True),
    )
    upstream_gradient = layer_backprop(
        output_gradient, second_preactivation, second_flipped_kernel, SECOND_DILATION
    )
    input_gradient = layer_backprop(
        upstream_gradient, first_preactivation, first_flipped_kernel, FIRST_DILATION
    )
    trial_shards = lax.axis_size("trial")
    neurons, trials, steps_count = spike_rates.shape
    neuron_blocks = spike_rates.reshape(trial_shards, neurons // trial_shards, trials, steps_count)
    partials = jnp.einsum(
        "jbil,cil->jibc", neuron_blocks, input_gradient, preferred_element_type=jnp.float32
    )
    arrived = lax.all_to_all(
        partials.astype(jnp.bfloat16), "trial", split_axis=0, concat_axis=0, tiled=True
    ).astype(partials.dtype)
    every_id = lax.all_gather(session_of, "trial", axis=0, tiled=True)
    total_trials = every_id.shape[0]
    flat_parts = arrived.reshape(total_trials, -1)
    session_list = jnp.arange(trial_shards, dtype=jnp.int32)
    first_trial = jnp.sum((every_id[None, :] < session_list[:, None]).astype(jnp.int32), axis=1)

    def add_offset(offset, running):
        position = first_trial + offset
        clipped = jnp.minimum(position, total_trials - 1)
        rows_here = jnp.take(flat_parts, clipped, axis=0)
        valid = (position < total_trials) & (jnp.take(every_id, clipped, axis=0) == session_list)
        return running + jnp.where(valid[:, None], rows_here, 0.0)

    start_sums = jnp.zeros((trial_shards, flat_parts.shape[1]), jnp.float32)
    summed = lax.fori_loop(0, MOST, add_offset, start_sums)
    return summed.reshape(trial_shards, neurons // trial_shards, input_gradient.shape[0]).astype(
        jnp.bfloat16
    )


MESH = pl.DeviceIdType.MESH
TRIALS_HERE = 2


def shifted(values, offset):
    if offset == 0:
        return values
    width = values.shape[1]
    rolled = pltpu.roll(values, width - offset, 1)
    lane = lax.broadcasted_iota(jnp.int32, values.shape, 1)
    return jnp.where(lane < width - offset, rolled, 0.0)


def split_pairs(source, index, target, halves):
    for chunk in range(halves):
        mixed = source[pl.ds(chunk * 256, 256), :]
        apart = jnp.dot(index, mixed, preferred_element_type=jnp.float32).astype(target.dtype)
        for trial in range(TRIALS_HERE):
            target[trial, pl.ds(chunk * 128, 128), :] = apart[trial * 128 : trial * 128 + 128]


def fused(
    shards,
    spikes_hbm,
    pre_one_in,
    pre_two_in,
    upstream_in,
    kernel_one_hbm,
    kernel_two_hbm,
    ids_in,
    out_ref,
    kernels,
    spikes_mixed,
    spikes,
    pre_one,
    pre_two,
    grad,
    slope_one,
    taps,
    own,
    wide,
    outgoing,
    diag_in,
    side_in,
    parts,
    arrived,
    ids_mine,
    ids_all,
    picks,
    total,
    load_sems,
    diag_send,
    diag_recv,
    side_send,
    side_recv,
    part_send,
    part_recv,
    id_send,
    id_recv,
):
    section = lax.axis_index("section")
    me = lax.axis_index("trial")
    along_x = section + 1 - 2 * (section % 2)
    along_y = (section + 2) % 4
    across = (along_x + 2) % 4
    rows = parts.shape[1] // shards
    spacings = (SECOND_DILATION, FIRST_DILATION)

    loads = [
        pltpu.make_async_copy(kernel_two_hbm, kernels.at[0], load_sems.at[0]),
        pltpu.make_async_copy(kernel_one_hbm, kernels.at[1], load_sems.at[1]),
        pltpu.make_async_copy(spikes_hbm, spikes_mixed, load_sems.at[2]),
    ]
    for load in loads:
        load.start()

    barrier = pltpu.get_barrier_semaphore()
    for partner in (along_x, along_y):
        pl.semaphore_signal(barrier, inc=1, device_id=(partner, me), device_id_type=MESH)
    for step in range(1, shards):
        peer = (me + step) % shards
        pl.semaphore_signal(barrier, inc=1, device_id=(section, peer), device_id_type=MESH)

    row = lax.broadcasted_iota(jnp.int32, (256, 256), 0)
    column = lax.broadcasted_iota(jnp.int32, (256, 256), 1)
    wanted = jnp.where(row < 128, 2 * row, 2 * row - 255)
    index = (column == wanted).astype(jnp.float32).astype(jnp.bfloat16)

    def diag_copies(unit):
        return [
            pltpu.make_async_remote_copy(
                src_ref=outgoing.at[unit, 2, pl.ds(128 * way, 128)],
                dst_ref=diag_in.at[unit, way],
                send_sem=diag_send.at[unit, way],
                recv_sem=diag_recv.at[unit, way],
                device_id=(partner, me),
                device_id_type=MESH,
            )
            for way, partner in enumerate((along_x, along_y))
        ]

    def side_copy(unit, way, half):
        partner = (along_x, along_y)[way]
        return pltpu.make_async_remote_copy(
            src_ref=outgoing.at[unit, way, pl.ds(128 * half, 128)],
            dst_ref=side_in.at[unit, way, pl.ds(128 * half, 128)],
            send_sem=side_send.at[unit, way, half],
            recv_sem=side_recv.at[unit, way, half],
            device_id=(partner, me),
            device_id_type=MESH,
        )

    def flow(layer, trial, upstream, slope):
        rounded = (upstream * slope).astype(jnp.bfloat16).astype(jnp.float32)
        for tap in range(3):
            taps[tap] = shifted(rounded, tap * spacings[layer]).astype(jnp.bfloat16)

    def product(layer, block, first, size):
        result = None
        for tap in range(3):
            weights = kernels[layer, tap, pl.ds(pl.multiple_of(block * 256 + first, 128), size), :]
            term = jnp.dot(weights, taps[tap], preferred_element_type=jnp.float32)
            result = term if result is None else result + term
        return result

    def compute(layer, unit, now):
        outgoing[unit, 2] = product(layer, across, 0, 256).astype(jnp.bfloat16)
        if now:
            for copy in diag_copies(unit):
                copy.start()
        outgoing[unit, 0, pl.ds(0, 128)] = product(layer, along_x, 0, 128).astype(jnp.bfloat16)
        outgoing[unit, 1, pl.ds(128, 128)] = product(layer, along_y, 128, 128).astype(jnp.bfloat16)
        if now:
            side_copy(unit, 0, 0).start()
            side_copy(unit, 1, 1).start()
        wide[unit, 0] = product(layer, along_y, 0, 128)
        wide[unit, 1] = product(layer, along_x, 128, 128)
        own[unit] = product(layer, section, 0, 256)

    def send(unit):
        for copy in diag_copies(unit):
            copy.start()
        side_copy(unit, 0, 0).start()
        side_copy(unit, 1, 1).start()

    def forward(unit):
        copies = diag_copies(unit)
        for way in range(2):
            copies[way].wait_recv()
            target, half = 1 - way, way
            joined = wide[unit, way] + diag_in[unit, way].astype(jnp.float32)
            outgoing[unit, target, pl.ds(128 * half, 128)] = joined.astype(jnp.bfloat16)
            side_copy(unit, target, half).start()

    def finish(unit, trial):
        for way in range(2):
            for half in range(2):
                side_copy(unit, way, half).wait_recv()
        back = own[unit] + side_in[unit, 0].astype(jnp.float32) + side_in[unit, 1].astype(jnp.float32)
        rounded = (grad[trial].astype(jnp.float32) + back).astype(jnp.bfloat16)
        grad[trial] = rounded
        return rounded

    def part_copy(trial, step):
        peer = (me + step) % shards
        return pltpu.make_async_remote_copy(
            src_ref=parts.at[trial, pl.ds(pl.multiple_of(peer * rows, rows), rows)],
            dst_ref=arrived.at[trial, pl.ds(pl.multiple_of(me * rows, rows), rows)],
            send_sem=part_send.at[trial, step],
            recv_sem=part_recv.at[trial, step],
            device_id=(section, peer),
            device_id_type=MESH,
        )

    def id_copy(step):
        peer = (me + step) % shards
        return pltpu.make_async_remote_copy(
            src_ref=ids_mine,
            dst_ref=ids_all.at[me],
            send_sem=id_send.at[step],
            recv_sem=id_recv.at[step],
            device_id=(section, peer),
            device_id_type=MESH,
        )

    def readin(trial, gradient):
        both = lax.dot_general(
            spikes[trial], gradient, (((1,), (1,)), ((), ())), preferred_element_type=jnp.float32
        )
        parts[trial] = both.astype(jnp.bfloat16)
        for step in range(1, shards):
            part_copy(trial, step).start()
        mine = pl.ds(pl.multiple_of(me * rows, rows), rows)
        arrived[trial, mine] = parts[trial, mine]

    def collect(trial):
        for step in range(1, shards):
            part_copy(trial, step).wait_recv()
        return jnp.dot(picks[trial], arrived[trial], preferred_element_type=jnp.float32)

    split_pairs(pre_two_in, index, pre_two, 2)
    split_pairs(upstream_in, index, grad, 2)
    flow(0, 0, grad[0].astype(jnp.float32), gelu_slope(pre_two[0]))
    loads[0].wait()
    pl.semaphore_wait(barrier, shards + 1)
    compute(0, 0, True)

    flow(0, 1, grad[1].astype(jnp.float32), gelu_slope(pre_two[1]))
    compute(0, 1, False)
    forward(0)
    send(1)

    top = lax.broadcasted_iota(jnp.int32, ids_mine.shape, 0)
    ids_mine[...] = jnp.where(top == 0, ids_in[0], ids_in[1])
    for step in range(1, shards):
        id_copy(step).start()
    ids_all[me] = ids_mine[...]

    split_pairs(pre_one_in, index, pre_one, 2)
    for trial in range(TRIALS_HERE):
        slope_one[trial] = gelu_slope(pre_one[trial])
    loads[1].wait()

    flow(1, 0, finish(0, 0).astype(jnp.float32), slope_one[0])
    compute(1, 2, False)
    forward(1)
    send(2)

    loads[2].wait()
    split_pairs(spikes_mixed, index, spikes, spikes_mixed.shape[0] // 256)

    flow(1, 1, finish(1, 1).astype(jnp.float32), slope_one[1])
    compute(1, 3, False)
    forward(2)
    send(3)

    for step in range(1, shards):
        id_copy(step).wait_recv()
    line = lax.broadcasted_iota(jnp.int32, (shards * rows, 128), 0)
    lane = lax.broadcasted_iota(jnp.int32, (shards * rows, 128), 1)
    same = (line % rows) == (lane % rows)
    session = line // rows
    per = 128 // rows
    for trial in range(TRIALS_HERE):
        for piece in range(shards * rows // 128):
            known = ids_all[piece * per, pl.ds(trial, 1), :]
            for slot in range(1, per):
                other = ids_all[piece * per + slot, pl.ds(trial, 1), :]
                known = jnp.where(lane[:1] < slot * rows, known, other)
            chosen = same & (session == known)
            picks[trial, :, pl.ds(piece * 128, 128)] = chosen.astype(jnp.float32).astype(jnp.bfloat16)

    readin(0, finish(2, 0))
    forward(3)
    readin(1, finish(3, 1))
    total[...] = collect(0)
    summed = total[...] + collect(1)
    out_ref[...] = summed.astype(jnp.bfloat16).reshape(out_ref.shape)

    for unit in range(4):
        for copy in diag_copies(unit):
            copy.wait_send()
        for way in range(2):
            for half in range(2):
                side_copy(unit, way, half).wait_send()
    for step in range(1, shards):
        for trial in range(TRIALS_HERE):
            part_copy(trial, step).wait_send()
        id_copy(step).wait_send()


def one_kernel(
    spike_rates,
    first_preactivation,
    second_preactivation,
    output_gradient,
    first_kernel,
    second_kernel,
    session_of,
):
    shards = lax.axis_size("trial")
    neurons, trials, steps = spike_rates.shape
    block = output_gradient.shape[0]
    rows = neurons // shards
    f32, bf16 = jnp.float32, jnp.bfloat16
    vmem = pl.BlockSpec(memory_space=pltpu.VMEM)
    anywhere = pl.BlockSpec(memory_space=pl.ANY)
    dma = pltpu.SemaphoreType.DMA

    def pairs(array):
        return array.reshape(array.shape[0] * trials, steps)

    return pl.pallas_call(
        functools.partial(fused, shards),
        out_shape=jax.ShapeDtypeStruct((shards, rows, block), bf16),
        in_specs=[
            anywhere,
            vmem,
            vmem,
            vmem,
            anywhere,
            anywhere,
            pl.BlockSpec(memory_space=pltpu.SMEM),
        ],
        out_specs=vmem,
        scratch_shapes=[
            pltpu.VMEM((2,) + first_kernel.shape, bf16),
            pltpu.VMEM((neurons * trials, steps), bf16),
            pltpu.VMEM((trials, neurons, steps), bf16),
            pltpu.VMEM((trials, block, steps), bf16),
            pltpu.VMEM((trials, block, steps), bf16),
            pltpu.VMEM((trials, block, steps), bf16),
            pltpu.VMEM((trials, block, steps), f32),
            pltpu.VMEM((3, block, steps), bf16),
            pltpu.VMEM((4, block, steps), f32),
            pltpu.VMEM((4, 2, block // 2, steps), f32),
            pltpu.VMEM((4, 3, block, steps), bf16),
            pltpu.VMEM((4, 2, block // 2, steps), bf16),
            pltpu.VMEM((4, 2, block, steps), bf16),
            pltpu.VMEM((trials, neurons, block), bf16),
            pltpu.VMEM((trials, neurons, block), bf16),
            pltpu.VMEM((8, 128), jnp.int32),
            pltpu.VMEM((shards, 8, 128), jnp.int32),
            pltpu.VMEM((trials, shards * rows, shards * rows), bf16),
            pltpu.VMEM((shards * rows, block), f32),
            dma((3,)),
            dma((4, 2)),
            dma((4, 2)),
            dma((4, 2, 2)),
            dma((4, 2, 2)),
            dma((trials, shards)),
            dma((trials, shards)),
            dma((shards,)),
            dma((shards,)),
        ],
        compiler_params=pltpu.CompilerParams(
            collective_id=0, has_side_effects=True, vmem_limit_bytes=48 * 1024 * 1024
        ),
        cost_estimate=pl.CostEstimate(
            flops=2_000_000_000, bytes_accessed=6_000_000, transcendentals=500_000
        ),
    )(
        pairs(spike_rates),
        pairs(first_preactivation),
        pairs(second_preactivation),
        pairs(output_gradient),
        first_kernel,
        second_kernel,
        session_of,
    )


def choose(mesh, spike_rates, *others):
    shards = mesh.shape["trial"]
    neurons, trials, steps = spike_rates.shape
    rows = neurons // shards
    fits = mesh.shape["section"] == 4 and trials == TRIALS_HERE and steps == 256
    fits = fits and others[0].shape[0] == 256 and neurons % 128 == 0 and rows in (16, 32, 64, 128)
    return (one_kernel if fits else body)(spike_rates, *others)


def solution(mesh):
    in_specs = (
        P(None, "trial", None),
        P("section", "trial", None),
        P("section", "trial", None),
        P("section", "trial", None),
        P(None, None, "section"),
        P(None, None, "section"),
        P("trial"),
    )
    out_specs = P(None, "trial", "section")
    run = functools.partial(choose, mesh)
    return jax.shard_map(run, mesh=mesh, in_specs=in_specs, out_specs=out_specs, check_vma=False)
```

```python
import functools
import math

import jax
import jax.numpy as jnp
from jax import lax
from jax.experimental import pallas as pl
from jax.experimental.pallas import tpu as pltpu
from jax.sharding import PartitionSpec as P

FIRST_DILATION = 32
SECOND_DILATION = 64
MOST = 6


def gelu_slope(preact):
    values = preact.astype(jnp.float32)
    normal_cdf = 0.5 * (1.0 + lax.erf(values * (1.0 / math.sqrt(2.0))))
    density = jnp.exp(-0.5 * values * values) * (1.0 / math.sqrt(2.0 * math.pi))
    return normal_cdf + values * density


def shift_ahead(values, offset):
    padding = [(0, 0)] * (values.ndim - 1) + [(0, offset)]
    return jnp.pad(values[..., offset:], padding)


def tap_sum(weights, flow_grad, spacing):
    running = None
    for kernel_tap in range(3):
        term_tap = lax.dot_general(
            weights[kernel_tap],
            flow_grad,
            (((1,), (0,)), ((), ())),
            preferred_element_type=jnp.float32,
        )
        if kernel_tap > 0:
            term_tap = shift_ahead(term_tap, kernel_tap * spacing)
        running = term_tap if running is None else running + term_tap
    return running


def layer_backprop(upstream, preact, turned, spacing):
    flow_grad = (upstream.astype(jnp.float32) * gelu_slope(preact)).astype(jnp.bfloat16)
    back_sum = tap_sum(turned, lax.all_gather(flow_grad, "section", axis=0, tiled=True), spacing)
    return (upstream.astype(jnp.float32) + back_sum).astype(jnp.bfloat16)


def body(
    spike_rates,
    first_preactivation,
    second_preactivation,
    output_gradient,
    first_kernel,
    second_kernel,
    session_of,
):
    first_flipped_kernel, second_flipped_kernel = (
        lax.all_to_all(first_kernel, "section", split_axis=1, concat_axis=2, tiled=True),
        lax.all_to_all(second_kernel, "section", split_axis=1, concat_axis=2, tiled=True),
    )
    upstream_gradient = layer_backprop(
        output_gradient, second_preactivation, second_flipped_kernel, SECOND_DILATION
    )
    input_gradient = layer_backprop(
        upstream_gradient, first_preactivation, first_flipped_kernel, FIRST_DILATION
    )
    trial_shards = lax.axis_size("trial")
    neurons, trials, steps_count = spike_rates.shape
    neuron_blocks = spike_rates.reshape(trial_shards, neurons // trial_shards, trials, steps_count)
    partials = jnp.einsum(
        "jbil,cil->jibc", neuron_blocks, input_gradient, preferred_element_type=jnp.float32
    )
    arrived = lax.all_to_all(
        partials.astype(jnp.bfloat16), "trial", split_axis=0, concat_axis=0, tiled=True
    ).astype(partials.dtype)
    every_id = lax.all_gather(session_of, "trial", axis=0, tiled=True)
    total_trials = every_id.shape[0]
    flat_parts = arrived.reshape(total_trials, -1)
    session_list = jnp.arange(trial_shards, dtype=jnp.int32)
    first_trial = jnp.sum((every_id[None, :] < session_list[:, None]).astype(jnp.int32), axis=1)

    def add_offset(offset, running):
        position = first_trial + offset
        clipped = jnp.minimum(position, total_trials - 1)
        rows_here = jnp.take(flat_parts, clipped, axis=0)
        valid = (position < total_trials) & (jnp.take(every_id, clipped, axis=0) == session_list)
        return running + jnp.where(valid[:, None], rows_here, 0.0)

    start_sums = jnp.zeros((trial_shards, flat_parts.shape[1]), jnp.float32)
    summed = lax.fori_loop(0, MOST, add_offset, start_sums)
    return summed.reshape(trial_shards, neurons // trial_shards, input_gradient.shape[0]).astype(
        jnp.bfloat16
    )


MESH = pl.DeviceIdType.MESH
TRIALS_HERE = 2


def shifted(values, offset):
    if offset == 0:
        return values
    width = values.shape[1]
    rolled = pltpu.roll(values, width - offset, 1)
    lane = lax.broadcasted_iota(jnp.int32, values.shape, 1)
    return jnp.where(lane < width - offset, rolled, 0.0)


def split_pairs(source, index, target, halves):
    for chunk in range(halves):
        mixed = source[pl.ds(chunk * 128, 128)].reshape(256, source.shape[2])
        apart = jnp.dot(index, mixed, preferred_element_type=jnp.float32).astype(target.dtype)
        for trial in range(TRIALS_HERE):
            target[trial, pl.ds(chunk * 128, 128), :] = apart[trial * 128 : trial * 128 + 128]


def fused(
    shards,
    spikes_hbm,
    pre_one_hbm,
    pre_two_hbm,
    upstream_hbm,
    kernel_one_hbm,
    kernel_two_hbm,
    ids_in,
    out_ref,
    kernels,
    pre_one_in,
    pre_two_in,
    upstream_in,
    spikes_mixed,
    spikes,
    pre_one,
    pre_two,
    grad,
    slope_one,
    taps,
    own,
    wide,
    outgoing,
    diag_in,
    side_in,
    parts,
    arrived,
    ids_mine,
    ids_all,
    picks,
    total,
    load_sems,
    diag_send,
    diag_recv,
    side_send,
    side_recv,
    part_send,
    part_recv,
    id_send,
    id_recv,
):
    section = lax.axis_index("section")
    me = lax.axis_index("trial")
    along_x = section + 1 - 2 * (section % 2)
    along_y = (section + 2) % 4
    across = (along_x + 2) % 4
    rows = parts.shape[2] // shards
    spacings = (SECOND_DILATION, FIRST_DILATION)
    far_first = sorted(range(1, shards), key=lambda step: abs(2 * step - shards))

    loads = [
        pltpu.make_async_copy(source, target, load_sems.at[place])
        for place, (source, target) in enumerate(
            (
                (pre_two_hbm, pre_two_in),
                (upstream_hbm, upstream_in),
                (kernel_two_hbm, kernels.at[0]),
                (pre_one_hbm, pre_one_in),
                (kernel_one_hbm, kernels.at[1]),
                (spikes_hbm, spikes_mixed),
            )
        )
    ]
    for load in loads:
        load.start()

    barrier = pltpu.get_barrier_semaphore()
    for partner in (along_x, along_y):
        pl.semaphore_signal(barrier, inc=1, device_id=(partner, me), device_id_type=MESH)
    for step in range(1, shards):
        peer = (me + step) % shards
        pl.semaphore_signal(barrier, inc=1, device_id=(section, peer), device_id_type=MESH)

    row = lax.broadcasted_iota(jnp.int32, (256, 256), 0)
    column = lax.broadcasted_iota(jnp.int32, (256, 256), 1)
    wanted = jnp.where(row < 128, 2 * row, 2 * row - 255)
    index = (column == wanted).astype(jnp.float32).astype(jnp.bfloat16)

    def diag_copy(unit, way, piece):
        partner = (along_x, along_y)[way]
        return pltpu.make_async_remote_copy(
            src_ref=outgoing.at[unit, 2, pl.ds(128 * piece + 64 * way, 64)],
            dst_ref=diag_in.at[unit, way, piece],
            send_sem=diag_send.at[unit, way, piece],
            recv_sem=diag_recv.at[unit, way, piece],
            device_id=(partner, me),
            device_id_type=MESH,
        )

    def side_copy(unit, way, piece, half):
        partner = (along_x, along_y)[way]
        lines = pl.ds(128 * piece + 64 * half, 64)
        return pltpu.make_async_remote_copy(
            src_ref=outgoing.at[unit, way, lines],
            dst_ref=side_in.at[unit, way, lines],
            send_sem=side_send.at[unit, way, piece, half],
            recv_sem=side_recv.at[unit, way, piece, half],
            device_id=(partner, me),
            device_id_type=MESH,
        )

    def flow(layer, lines, upstream, slope):
        rounded = (upstream * slope).astype(jnp.bfloat16).astype(jnp.float32)
        for tap in range(3):
            taps[tap, lines] = shifted(rounded, tap * spacings[layer]).astype(jnp.bfloat16)

    def product(layer, target):
        result = None
        for tap in range(3):
            weights = kernels[layer, tap, pl.ds(pl.multiple_of(target * 256, 256), 256), :]
            term = jnp.dot(weights, taps[tap], preferred_element_type=jnp.float32)
            result = term if result is None else result + term
        return result

    def compute(layer, unit):
        outgoing[unit, 2] = product(layer, across).astype(jnp.bfloat16)
        for piece in range(2):
            for way in range(2):
                diag_copy(unit, way, piece).start()
        for way, partner in enumerate((along_x, along_y)):
            result = product(layer, partner)
            for piece in range(2):
                near, far = 128 * piece + 64 * way, 128 * piece + 64 * (1 - way)
                outgoing[unit, way, pl.ds(near, 64)] = result[near : near + 64].astype(jnp.bfloat16)
                wide[unit, 1 - way, piece] = result[far : far + 64]
                side_copy(unit, way, piece, way).start()
        own[unit] = product(layer, section)

    def forward(unit, piece):
        for way in range(2):
            diag_copy(unit, way, piece).wait_recv()
            joined = wide[unit, way, piece] + diag_in[unit, way, piece].astype(jnp.float32)
            lines = pl.ds(128 * piece + 64 * way, 64)
            outgoing[unit, 1 - way, lines] = joined.astype(jnp.bfloat16)
            side_copy(unit, 1 - way, piece, way).start()

    def finish(unit, trial, piece):
        for way in range(2):
            for half in range(2):
                side_copy(unit, way, piece, half).wait_recv()
        lines = pl.ds(128 * piece, 128)
        first, second = side_in[unit, 0, lines], side_in[unit, 1, lines]
        back = own[unit, lines] + first.astype(jnp.float32) + second.astype(jnp.float32)
        rounded = (grad[trial, lines].astype(jnp.float32) + back).astype(jnp.bfloat16)
        grad[trial, lines] = rounded
        return rounded

    def turn(unit, trial):
        for piece in range(2):
            lines = pl.ds(128 * piece, 128)
            upstream = finish(unit, trial, piece).astype(jnp.float32)
            flow(1, lines, upstream, slope_one[trial, lines])

    def part_copy(trial, piece, step):
        peer = (me + step) % shards
        return pltpu.make_async_remote_copy(
            src_ref=parts.at[trial, piece, pl.ds(pl.multiple_of(peer * rows, rows), rows)],
            dst_ref=arrived.at[trial, piece, pl.ds(pl.multiple_of(me * rows, rows), rows)],
            send_sem=part_send.at[trial, piece, step],
            recv_sem=part_recv.at[trial, piece, step],
            device_id=(section, peer),
            device_id_type=MESH,
        )

    def id_copy(step):
        peer = (me + step) % shards
        return pltpu.make_async_remote_copy(
            src_ref=ids_mine,
            dst_ref=ids_all.at[me],
            send_sem=id_send.at[step],
            recv_sem=id_recv.at[step],
            device_id=(section, peer),
            device_id_type=MESH,
        )

    def readin(trial, piece, gradient):
        both = lax.dot_general(
            spikes[trial], gradient, (((1,), (1,)), ((), ())), preferred_element_type=jnp.float32
        )
        parts[trial, piece] = both.astype(jnp.bfloat16)
        for step in far_first:
            part_copy(trial, piece, step).start()
        mine = pl.ds(pl.multiple_of(me * rows, rows), rows)
        arrived[trial, piece, mine] = parts[trial, piece, mine]

    def collect(trial, piece):
        for step in range(1, shards):
            part_copy(trial, piece, step).wait_recv()
        return jnp.dot(picks[trial], arrived[trial, piece], preferred_element_type=jnp.float32)

    whole = pl.ds(0, 256)
    loads[0].wait()
    split_pairs(pre_two_in, index, pre_two, 2)
    loads[1].wait()
    split_pairs(upstream_in, index, grad, 2)
    flow(0, whole, grad[0].astype(jnp.float32), gelu_slope(pre_two[0]))
    loads[2].wait()
    pl.semaphore_wait(barrier, shards + 1)
    compute(0, 0)

    flow(0, whole, grad[1].astype(jnp.float32), gelu_slope(pre_two[1]))
    forward(0, 0)
    forward(0, 1)
    compute(0, 1)

    top = lax.broadcasted_iota(jnp.int32, ids_mine.shape, 0)
    ids_mine[...] = jnp.where(top == 0, ids_in[0], ids_in[1])
    for step in range(1, shards):
        id_copy(step).start()
    ids_all[me] = ids_mine[...]

    loads[3].wait()
    split_pairs(pre_one_in, index, pre_one, 2)
    for trial in range(TRIALS_HERE):
        slope_one[trial] = gelu_slope(pre_one[trial])
    forward(1, 0)
    forward(1, 1)

    loads[4].wait()
    turn(0, 0)
    compute(1, 2)

    turn(1, 1)
    forward(2, 0)
    forward(2, 1)
    compute(1, 3)

    loads[5].wait()
    split_pairs(spikes_mixed, index, spikes, spikes_mixed.shape[0] // 128)

    readin(0, 0, finish(2, 0, 0))
    forward(3, 0)
    forward(3, 1)
    readin(0, 1, finish(2, 0, 1))

    for step in range(1, shards):
        id_copy(step).wait_recv()
    line = lax.broadcasted_iota(jnp.int32, (shards * rows, 128), 0)
    lane = lax.broadcasted_iota(jnp.int32, (shards * rows, 128), 1)
    same = (line % rows) == (lane % rows)
    session = line // rows
    per = 128 // rows
    for trial in range(TRIALS_HERE):
        for piece in range(shards * rows // 128):
            known = ids_all[piece * per, pl.ds(trial, 1), :]
            for slot in range(1, per):
                other = ids_all[piece * per + slot, pl.ds(trial, 1), :]
                known = jnp.where(lane[:1] < slot * rows, known, other)
            chosen = same & (session == known)
            picks[trial, :, pl.ds(piece * 128, 128)] = chosen.astype(jnp.float32).astype(jnp.bfloat16)

    for piece in range(2):
        readin(1, piece, finish(3, 1, piece))
    for piece in range(2):
        total[piece] = collect(0, piece)
    for piece in range(2):
        summed = (total[piece] + collect(1, piece)).astype(jnp.bfloat16)
        out_ref[:, :, pl.ds(128 * piece, 128)] = summed.reshape(shards, rows, 128)

    for piece in range(2):
        for unit in range(4):
            for way in range(2):
                diag_copy(unit, way, piece).wait_send()
                for half in range(2):
                    side_copy(unit, way, piece, half).wait_send()
        for step in range(1, shards):
            for trial in range(TRIALS_HERE):
                part_copy(trial, piece, step).wait_send()
    for step in range(1, shards):
        id_copy(step).wait_send()


def one_kernel(
    spike_rates,
    first_preactivation,
    second_preactivation,
    output_gradient,
    first_kernel,
    second_kernel,
    session_of,
):
    shards = lax.axis_size("trial")
    neurons, trials, steps = spike_rates.shape
    block = output_gradient.shape[0]
    rows = neurons // shards
    f32, bf16 = jnp.float32, jnp.bfloat16
    vmem = pl.BlockSpec(memory_space=pltpu.VMEM)
    hbm = pl.BlockSpec(memory_space=pltpu.HBM)
    dma = pltpu.SemaphoreType.DMA

    return pl.pallas_call(
        functools.partial(fused, shards),
        out_shape=jax.ShapeDtypeStruct((shards, rows, block), bf16),
        in_specs=[
            hbm,
            hbm,
            hbm,
            hbm,
            hbm,
            hbm,
            pl.BlockSpec(memory_space=pltpu.SMEM),
        ],
        out_specs=vmem,
        scratch_shapes=[
            pltpu.VMEM((2,) + first_kernel.shape, bf16),
            pltpu.VMEM((block, trials, steps), bf16),
            pltpu.VMEM((block, trials, steps), bf16),
            pltpu.VMEM((block, trials, steps), bf16),
            pltpu.VMEM((neurons, trials, steps), bf16),
            pltpu.VMEM((trials, neurons, steps), bf16),
            pltpu.VMEM((trials, block, steps), bf16),
            pltpu.VMEM((trials, block, steps), bf16),
            pltpu.VMEM((trials, block, steps), bf16),
            pltpu.VMEM((trials, block, steps), f32),
            pltpu.VMEM((3, block, steps), bf16),
            pltpu.VMEM((4, block, steps), f32),
            pltpu.VMEM((4, 2, 2, block // 4, steps), f32),
            pltpu.VMEM((4, 3, block, steps), bf16),
            pltpu.VMEM((4, 2, 2, block // 4, steps), bf16),
            pltpu.VMEM((4, 2, block, steps), bf16),
            pltpu.VMEM((trials, 2, neurons, block // 2), bf16),
            pltpu.VMEM((trials, 2, neurons, block // 2), bf16),
            pltpu.VMEM((8, 128), jnp.int32),
            pltpu.VMEM((shards, 8, 128), jnp.int32),
            pltpu.VMEM((trials, shards * rows, shards * rows), bf16),
            pltpu.VMEM((2, shards * rows, block // 2), f32),
            dma((6,)),
            dma((4, 2, 2)),
            dma((4, 2, 2)),
            dma((4, 2, 2, 2)),
            dma((4, 2, 2, 2)),
            dma((trials, 2, shards)),
            dma((trials, 2, shards)),
            dma((shards,)),
            dma((shards,)),
        ],
        compiler_params=pltpu.CompilerParams(
            collective_id=0, has_side_effects=True, vmem_limit_bytes=63 * 1024 * 1024
        ),
        cost_estimate=pl.CostEstimate(
            flops=2_000_000_000, bytes_accessed=6_000_000, transcendentals=500_000
        ),
    )(
        spike_rates,
        first_preactivation,
        second_preactivation,
        output_gradient,
        first_kernel,
        second_kernel,
        session_of,
    )


def choose(mesh, spike_rates, *others):
    shards = mesh.shape["trial"]
    neurons, trials, steps = spike_rates.shape
    rows = neurons // shards
    fits = mesh.shape["section"] == 4 and trials == TRIALS_HERE and steps == 256
    fits = fits and others[0].shape[0] == 256 and neurons % 128 == 0 and rows in (16, 32, 64, 128)
    return (one_kernel if fits else body)(spike_rates, *others)


def solution(mesh):
    in_specs = (
        P(None, "trial", None),
        P("section", "trial", None),
        P("section", "trial", None),
        P("section", "trial", None),
        P(None, None, "section"),
        P(None, None, "section"),
        P("trial"),
    )
    out_specs = P(None, "trial", "section")
    run = functools.partial(choose, mesh)
    return jax.shard_map(run, mesh=mesh, in_specs=in_specs, out_specs=out_specs, check_vma=False)
```

```python
import functools
import math

import jax
import jax.numpy as jnp
from jax import lax
from jax.experimental import pallas as pl
from jax.experimental.pallas import tpu as pltpu
from jax.sharding import PartitionSpec as P

FIRST_DILATION = 32
SECOND_DILATION = 64
MOST = 6


def gelu_slope(preact):
    values = preact.astype(jnp.float32)
    normal_cdf = 0.5 * (1.0 + lax.erf(values * (1.0 / math.sqrt(2.0))))
    density = jnp.exp(-0.5 * values * values) * (1.0 / math.sqrt(2.0 * math.pi))
    return normal_cdf + values * density


def shift_ahead(values, offset):
    padding = [(0, 0)] * (values.ndim - 1) + [(0, offset)]
    return jnp.pad(values[..., offset:], padding)


def tap_sum(weights, flow_grad, spacing):
    running = None
    for kernel_tap in range(3):
        term_tap = lax.dot_general(
            weights[kernel_tap],
            flow_grad,
            (((1,), (0,)), ((), ())),
            preferred_element_type=jnp.float32,
        )
        if kernel_tap > 0:
            term_tap = shift_ahead(term_tap, kernel_tap * spacing)
        running = term_tap if running is None else running + term_tap
    return running


def layer_backprop(upstream, preact, turned, spacing):
    flow_grad = (upstream.astype(jnp.float32) * gelu_slope(preact)).astype(jnp.bfloat16)
    back_sum = tap_sum(turned, lax.all_gather(flow_grad, "section", axis=0, tiled=True), spacing)
    return (upstream.astype(jnp.float32) + back_sum).astype(jnp.bfloat16)


def body(
    spike_rates,
    first_preactivation,
    second_preactivation,
    output_gradient,
    first_kernel,
    second_kernel,
    session_of,
):
    first_flipped_kernel, second_flipped_kernel = (
        lax.all_to_all(first_kernel, "section", split_axis=1, concat_axis=2, tiled=True),
        lax.all_to_all(second_kernel, "section", split_axis=1, concat_axis=2, tiled=True),
    )
    upstream_gradient = layer_backprop(
        output_gradient, second_preactivation, second_flipped_kernel, SECOND_DILATION
    )
    input_gradient = layer_backprop(
        upstream_gradient, first_preactivation, first_flipped_kernel, FIRST_DILATION
    )
    trial_shards = lax.axis_size("trial")
    neurons, trials, steps_count = spike_rates.shape
    neuron_blocks = spike_rates.reshape(trial_shards, neurons // trial_shards, trials, steps_count)
    partials = jnp.einsum(
        "jbil,cil->jibc", neuron_blocks, input_gradient, preferred_element_type=jnp.float32
    )
    arrived = lax.all_to_all(
        partials.astype(jnp.bfloat16), "trial", split_axis=0, concat_axis=0, tiled=True
    ).astype(partials.dtype)
    every_id = lax.all_gather(session_of, "trial", axis=0, tiled=True)
    total_trials = every_id.shape[0]
    flat_parts = arrived.reshape(total_trials, -1)
    session_list = jnp.arange(trial_shards, dtype=jnp.int32)
    first_trial = jnp.sum((every_id[None, :] < session_list[:, None]).astype(jnp.int32), axis=1)

    def add_offset(offset, running):
        position = first_trial + offset
        clipped = jnp.minimum(position, total_trials - 1)
        rows_here = jnp.take(flat_parts, clipped, axis=0)
        valid = (position < total_trials) & (jnp.take(every_id, clipped, axis=0) == session_list)
        return running + jnp.where(valid[:, None], rows_here, 0.0)

    start_sums = jnp.zeros((trial_shards, flat_parts.shape[1]), jnp.float32)
    summed = lax.fori_loop(0, MOST, add_offset, start_sums)
    return summed.reshape(trial_shards, neurons // trial_shards, input_gradient.shape[0]).astype(
        jnp.bfloat16
    )


MESH = pl.DeviceIdType.MESH
TRIALS_HERE = 2


def shifted(values, offset):
    if offset == 0:
        return values
    width = values.shape[1]
    rolled = pltpu.roll(values, width - offset, 1)
    lane = lax.broadcasted_iota(jnp.int32, values.shape, 1)
    return jnp.where(lane < width - offset, rolled, 0.0)


def split_pairs(source, index, target, halves):
    for chunk in range(halves):
        mixed = source[pl.ds(chunk * 128, 128)].reshape(256, source.shape[2])
        apart = jnp.dot(index, mixed, preferred_element_type=jnp.float32).astype(target.dtype)
        for trial in range(TRIALS_HERE):
            target[trial, pl.ds(chunk * 128, 128), :] = apart[trial * 128 : trial * 128 + 128]


def fused(
    shards,
    spikes_hbm,
    pre_one_hbm,
    pre_two_hbm,
    upstream_hbm,
    kernel_one_hbm,
    kernel_two_hbm,
    ids_in,
    out_ref,
    kernels,
    pre_one_in,
    pre_two_in,
    upstream_in,
    spikes_mixed,
    spikes,
    pre_one,
    pre_two,
    grad,
    slope_one,
    taps,
    own,
    wide,
    outgoing,
    diag_in,
    side_in,
    parts,
    arrived,
    ids_mine,
    ids_all,
    picks,
    total,
    load_sems,
    diag_send,
    diag_recv,
    side_send,
    side_recv,
    part_send,
    part_recv,
    id_send,
    id_recv,
):
    section = lax.axis_index("section")
    me = lax.axis_index("trial")
    along_x = section + 1 - 2 * (section % 2)
    along_y = (section + 2) % 4
    across = (along_x + 2) % 4
    rows = parts.shape[2] // shards
    spacings = (SECOND_DILATION, FIRST_DILATION)
    far_first = sorted(range(1, shards), key=lambda step: abs(2 * step - shards))

    loads = [
        pltpu.make_async_copy(source, target, load_sems.at[place])
        for place, (source, target) in enumerate(
            (
                (pre_two_hbm, pre_two_in),
                (upstream_hbm, upstream_in),
                (kernel_two_hbm, kernels.at[0]),
                (pre_one_hbm, pre_one_in),
                (kernel_one_hbm, kernels.at[1]),
                (spikes_hbm, spikes_mixed),
            )
        )
    ]
    for load in loads:
        load.start()

    barrier = pltpu.get_barrier_semaphore()
    for partner in (along_x, along_y):
        pl.semaphore_signal(barrier, inc=1, device_id=(partner, me), device_id_type=MESH)
    for step in range(1, shards):
        peer = (me + step) % shards
        pl.semaphore_signal(barrier, inc=1, device_id=(section, peer), device_id_type=MESH)

    row = lax.broadcasted_iota(jnp.int32, (256, 256), 0)
    column = lax.broadcasted_iota(jnp.int32, (256, 256), 1)
    wanted = jnp.where(row < 128, 2 * row, 2 * row - 255)
    index = (column == wanted).astype(jnp.float32).astype(jnp.bfloat16)

    def diag_copy(unit, way, piece):
        partner = (along_x, along_y)[way]
        return pltpu.make_async_remote_copy(
            src_ref=outgoing.at[unit, 2, pl.ds(128 * piece + 64 * way, 64)],
            dst_ref=diag_in.at[unit, way, piece],
            send_sem=diag_send.at[unit, way, piece],
            recv_sem=diag_recv.at[unit, way, piece],
            device_id=(partner, me),
            device_id_type=MESH,
        )

    def side_copy(unit, way, piece, half):
        partner = (along_x, along_y)[way]
        lines = pl.ds(128 * piece + 64 * half, 64)
        return pltpu.make_async_remote_copy(
            src_ref=outgoing.at[unit, way, lines],
            dst_ref=side_in.at[unit, way, lines],
            send_sem=side_send.at[unit, way, piece, half],
            recv_sem=side_recv.at[unit, way, piece, half],
            device_id=(partner, me),
            device_id_type=MESH,
        )

    def flow(layer, lines, upstream, slope):
        rounded = (upstream * slope).astype(jnp.bfloat16).astype(jnp.float32)
        for tap in range(3):
            taps[tap, lines] = shifted(rounded, tap * spacings[layer]).astype(jnp.bfloat16)

    def product(layer, target):
        result = None
        for tap in range(3):
            weights = kernels[layer, tap, pl.ds(pl.multiple_of(target * 256, 256), 256), :]
            term = jnp.dot(weights, taps[tap], preferred_element_type=jnp.float32)
            result = term if result is None else result + term
        return result

    def compute(layer, unit):
        outgoing[unit, 2] = product(layer, across).astype(jnp.bfloat16)
        for way in range(2):
            diag_copy(unit, way, 0).start()
        for way, partner in enumerate((along_x, along_y)):
            result = product(layer, partner)
            for piece in range(2):
                near, far = 128 * piece + 64 * way, 128 * piece + 64 * (1 - way)
                outgoing[unit, way, pl.ds(near, 64)] = result[near : near + 64].astype(jnp.bfloat16)
                wide[unit, 1 - way, piece] = result[far : far + 64]
            side_copy(unit, way, 0, way).start()
            diag_copy(unit, way, 1).start()
            side_copy(unit, way, 1, way).start()
        own[unit] = product(layer, section)

    def forward(unit, piece):
        for way in range(2):
            diag_copy(unit, way, piece).wait_recv()
            joined = wide[unit, way, piece] + diag_in[unit, way, piece].astype(jnp.float32)
            lines = pl.ds(128 * piece + 64 * way, 64)
            outgoing[unit, 1 - way, lines] = joined.astype(jnp.bfloat16)
            side_copy(unit, 1 - way, piece, way).start()

    def finish(unit, trial, piece):
        for way in range(2):
            for half in range(2):
                side_copy(unit, way, piece, half).wait_recv()
        lines = pl.ds(128 * piece, 128)
        first, second = side_in[unit, 0, lines], side_in[unit, 1, lines]
        back = own[unit, lines] + first.astype(jnp.float32) + second.astype(jnp.float32)
        rounded = (grad[trial, lines].astype(jnp.float32) + back).astype(jnp.bfloat16)
        grad[trial, lines] = rounded
        return rounded

    def turn(unit, trial):
        for piece in range(2):
            lines = pl.ds(128 * piece, 128)
            upstream = finish(unit, trial, piece).astype(jnp.float32)
            flow(1, lines, upstream, slope_one[trial, lines])

    def part_copy(trial, piece, step):
        peer = (me + step) % shards
        return pltpu.make_async_remote_copy(
            src_ref=parts.at[trial, piece, pl.ds(pl.multiple_of(peer * rows, rows), rows)],
            dst_ref=arrived.at[trial, piece, pl.ds(pl.multiple_of(me * rows, rows), rows)],
            send_sem=part_send.at[trial, piece, step],
            recv_sem=part_recv.at[trial, piece, step],
            device_id=(section, peer),
            device_id_type=MESH,
        )

    def id_copy(step):
        peer = (me + step) % shards
        return pltpu.make_async_remote_copy(
            src_ref=ids_mine,
            dst_ref=ids_all.at[me],
            send_sem=id_send.at[step],
            recv_sem=id_recv.at[step],
            device_id=(section, peer),
            device_id_type=MESH,
        )

    def readin(trial, piece, gradient):
        both = lax.dot_general(
            spikes[trial], gradient, (((1,), (1,)), ((), ())), preferred_element_type=jnp.float32
        )
        parts[trial, piece] = both.astype(jnp.bfloat16)
        for step in far_first:
            part_copy(trial, piece, step).start()
        mine = pl.ds(pl.multiple_of(me * rows, rows), rows)
        arrived[trial, piece, mine] = parts[trial, piece, mine]

    def collect(trial, piece):
        for step in range(1, shards):
            part_copy(trial, piece, step).wait_recv()
        return jnp.dot(picks[trial], arrived[trial, piece], preferred_element_type=jnp.float32)

    whole = pl.ds(0, 256)
    loads[0].wait()
    split_pairs(pre_two_in, index, pre_two, 2)
    loads[1].wait()
    split_pairs(upstream_in, index, grad, 2)
    flow(0, whole, grad[0].astype(jnp.float32), gelu_slope(pre_two[0]))
    loads[2].wait()
    pl.semaphore_wait(barrier, shards + 1)
    compute(0, 0)

    flow(0, whole, grad[1].astype(jnp.float32), gelu_slope(pre_two[1]))
    forward(0, 0)
    top = lax.broadcasted_iota(jnp.int32, ids_mine.shape, 0)
    ids_mine[...] = jnp.where(top == 0, ids_in[0], ids_in[1])
    for step in range(1, shards):
        id_copy(step).start()
    ids_all[me] = ids_mine[...]
    loads[3].wait()
    split_pairs(pre_one_in, index, pre_one, 2)
    slope_one[0] = gelu_slope(pre_one[0])
    forward(0, 1)
    compute(0, 1)

    slope_one[1] = gelu_slope(pre_one[1])
    loads[4].wait()
    turn(0, 0)
    compute(1, 2)
    forward(1, 0)
    loads[5].wait()
    split_pairs(spikes_mixed, index, spikes, spikes_mixed.shape[0] // 128)
    forward(2, 0)
    forward(2, 1)
    forward(1, 1)

    readin(0, 0, finish(2, 0, 0))
    readin(0, 1, finish(2, 0, 1))
    turn(1, 1)
    compute(1, 3)
    forward(3, 0)
    forward(3, 1)

    for step in range(1, shards):
        id_copy(step).wait_recv()
    line = lax.broadcasted_iota(jnp.int32, (shards * rows, 128), 0)
    lane = lax.broadcasted_iota(jnp.int32, (shards * rows, 128), 1)
    same = (line % rows) == (lane % rows)
    session = line // rows
    per = 128 // rows
    for trial in range(TRIALS_HERE):
        for piece in range(shards * rows // 128):
            known = ids_all[piece * per, pl.ds(trial, 1), :]
            for slot in range(1, per):
                other = ids_all[piece * per + slot, pl.ds(trial, 1), :]
                known = jnp.where(lane[:1] < slot * rows, known, other)
            chosen = same & (session == known)
            picks[trial, :, pl.ds(piece * 128, 128)] = chosen.astype(jnp.float32).astype(jnp.bfloat16)

    for piece in range(2):
        readin(1, piece, finish(3, 1, piece))
    for piece in range(2):
        total[piece] = collect(0, piece)
    for piece in range(2):
        summed = (total[piece] + collect(1, piece)).astype(jnp.bfloat16)
        out_ref[:, :, pl.ds(128 * piece, 128)] = summed.reshape(shards, rows, 128)

    for piece in range(2):
        for unit in range(4):
            for way in range(2):
                diag_copy(unit, way, piece).wait_send()
                for half in range(2):
                    side_copy(unit, way, piece, half).wait_send()
        for step in range(1, shards):
            for trial in range(TRIALS_HERE):
                part_copy(trial, piece, step).wait_send()
    for step in range(1, shards):
        id_copy(step).wait_send()


def one_kernel(
    spike_rates,
    first_preactivation,
    second_preactivation,
    output_gradient,
    first_kernel,
    second_kernel,
    session_of,
):
    shards = lax.axis_size("trial")
    neurons, trials, steps = spike_rates.shape
    block = output_gradient.shape[0]
    rows = neurons // shards
    f32, bf16 = jnp.float32, jnp.bfloat16
    vmem = pl.BlockSpec(memory_space=pltpu.VMEM)
    hbm = pl.BlockSpec(memory_space=pltpu.HBM)
    dma = pltpu.SemaphoreType.DMA

    return pl.pallas_call(
        functools.partial(fused, shards),
        out_shape=jax.ShapeDtypeStruct((shards, rows, block), bf16),
        in_specs=[
            hbm,
            hbm,
            hbm,
            hbm,
            hbm,
            hbm,
            pl.BlockSpec(memory_space=pltpu.SMEM),
        ],
        out_specs=vmem,
        scratch_shapes=[
            pltpu.VMEM((2,) + first_kernel.shape, bf16),
            pltpu.VMEM((block, trials, steps), bf16),
            pltpu.VMEM((block, trials, steps), bf16),
            pltpu.VMEM((block, trials, steps), bf16),
            pltpu.VMEM((neurons, trials, steps), bf16),
            pltpu.VMEM((trials, neurons, steps), bf16),
            pltpu.VMEM((trials, block, steps), bf16),
            pltpu.VMEM((trials, block, steps), bf16),
            pltpu.VMEM((trials, block, steps), bf16),
            pltpu.VMEM((trials, block, steps), f32),
            pltpu.VMEM((3, block, steps), bf16),
            pltpu.VMEM((4, block, steps), f32),
            pltpu.VMEM((4, 2, 2, block // 4, steps), f32),
            pltpu.VMEM((4, 3, block, steps), bf16),
            pltpu.VMEM((4, 2, 2, block // 4, steps), bf16),
            pltpu.VMEM((4, 2, block, steps), bf16),
            pltpu.VMEM((trials, 2, neurons, block // 2), bf16),
            pltpu.VMEM((trials, 2, neurons, block // 2), bf16),
            pltpu.VMEM((8, 128), jnp.int32),
            pltpu.VMEM((shards, 8, 128), jnp.int32),
            pltpu.VMEM((trials, shards * rows, shards * rows), bf16),
            pltpu.VMEM((2, shards * rows, block // 2), f32),
            dma((6,)),
            dma((4, 2, 2)),
            dma((4, 2, 2)),
            dma((4, 2, 2, 2)),
            dma((4, 2, 2, 2)),
            dma((trials, 2, shards)),
            dma((trials, 2, shards)),
            dma((shards,)),
            dma((shards,)),
        ],
        compiler_params=pltpu.CompilerParams(
            collective_id=0, has_side_effects=True, vmem_limit_bytes=63 * 1024 * 1024
        ),
        cost_estimate=pl.CostEstimate(
            flops=2_000_000_000, bytes_accessed=6_000_000, transcendentals=500_000
        ),
    )(
        spike_rates,
        first_preactivation,
        second_preactivation,
        output_gradient,
        first_kernel,
        second_kernel,
        session_of,
    )


def choose(mesh, spike_rates, *others):
    shards = mesh.shape["trial"]
    neurons, trials, steps = spike_rates.shape
    rows = neurons // shards
    fits = mesh.shape["section"] == 4 and trials == TRIALS_HERE and steps == 256
    fits = fits and others[0].shape[0] == 256 and neurons % 128 == 0 and rows in (16, 32, 64, 128)
    return (one_kernel if fits else body)(spike_rates, *others)


def solution(mesh):
    in_specs = (
        P(None, "trial", None),
        P("section", "trial", None),
        P("section", "trial", None),
        P("section", "trial", None),
        P(None, None, "section"),
        P(None, None, "section"),
        P("trial"),
    )
    out_specs = P(None, "trial", "section")
    run = functools.partial(choose, mesh)
    return jax.shard_map(run, mesh=mesh, in_specs=in_specs, out_specs=out_specs, check_vma=False)
```

```python
import functools
import math

import jax
import jax.numpy as jnp
from jax import lax
from jax.experimental import pallas as pl
from jax.experimental.pallas import tpu as pltpu
from jax.sharding import PartitionSpec as P

FIRST_DILATION = 32
SECOND_DILATION = 64
MOST = 6


def gelu_slope(preact):
    values = preact.astype(jnp.float32)
    normal_cdf = 0.5 * (1.0 + lax.erf(values * (1.0 / math.sqrt(2.0))))
    density = jnp.exp(-0.5 * values * values) * (1.0 / math.sqrt(2.0 * math.pi))
    return normal_cdf + values * density


def shift_ahead(values, offset):
    padding = [(0, 0)] * (values.ndim - 1) + [(0, offset)]
    return jnp.pad(values[..., offset:], padding)


def tap_sum(weights, flow_grad, spacing):
    running = None
    for kernel_tap in range(3):
        term_tap = lax.dot_general(
            weights[kernel_tap],
            flow_grad,
            (((1,), (0,)), ((), ())),
            preferred_element_type=jnp.float32,
        )
        if kernel_tap > 0:
            term_tap = shift_ahead(term_tap, kernel_tap * spacing)
        running = term_tap if running is None else running + term_tap
    return running


def layer_backprop(upstream, preact, turned, spacing):
    flow_grad = (upstream.astype(jnp.float32) * gelu_slope(preact)).astype(jnp.bfloat16)
    back_sum = tap_sum(turned, lax.all_gather(flow_grad, "section", axis=0, tiled=True), spacing)
    return (upstream.astype(jnp.float32) + back_sum).astype(jnp.bfloat16)


def body(
    spike_rates,
    first_preactivation,
    second_preactivation,
    output_gradient,
    first_kernel,
    second_kernel,
    session_of,
):
    first_flipped_kernel, second_flipped_kernel = (
        lax.all_to_all(first_kernel, "section", split_axis=1, concat_axis=2, tiled=True),
        lax.all_to_all(second_kernel, "section", split_axis=1, concat_axis=2, tiled=True),
    )
    upstream_gradient = layer_backprop(
        output_gradient, second_preactivation, second_flipped_kernel, SECOND_DILATION
    )
    input_gradient = layer_backprop(
        upstream_gradient, first_preactivation, first_flipped_kernel, FIRST_DILATION
    )
    trial_shards = lax.axis_size("trial")
    neurons, trials, steps_count = spike_rates.shape
    neuron_blocks = spike_rates.reshape(trial_shards, neurons // trial_shards, trials, steps_count)
    partials = jnp.einsum(
        "jbil,cil->jibc", neuron_blocks, input_gradient, preferred_element_type=jnp.float32
    )
    arrived = lax.all_to_all(
        partials.astype(jnp.bfloat16), "trial", split_axis=0, concat_axis=0, tiled=True
    ).astype(partials.dtype)
    every_id = lax.all_gather(session_of, "trial", axis=0, tiled=True)
    total_trials = every_id.shape[0]
    flat_parts = arrived.reshape(total_trials, -1)
    session_list = jnp.arange(trial_shards, dtype=jnp.int32)
    first_trial = jnp.sum((every_id[None, :] < session_list[:, None]).astype(jnp.int32), axis=1)

    def add_offset(offset, running):
        position = first_trial + offset
        clipped = jnp.minimum(position, total_trials - 1)
        rows_here = jnp.take(flat_parts, clipped, axis=0)
        valid = (position < total_trials) & (jnp.take(every_id, clipped, axis=0) == session_list)
        return running + jnp.where(valid[:, None], rows_here, 0.0)

    start_sums = jnp.zeros((trial_shards, flat_parts.shape[1]), jnp.float32)
    summed = lax.fori_loop(0, MOST, add_offset, start_sums)
    return summed.reshape(trial_shards, neurons // trial_shards, input_gradient.shape[0]).astype(
        jnp.bfloat16
    )


MESH = pl.DeviceIdType.MESH
TRIALS_HERE = 2


def shifted(values, offset):
    if offset == 0:
        return values
    width = values.shape[1]
    rolled = pltpu.roll(values, width - offset, 1)
    lane = lax.broadcasted_iota(jnp.int32, values.shape, 1)
    return jnp.where(lane < width - offset, rolled, 0.0)


def split_pairs(source, index, target, halves):
    for chunk in range(halves):
        mixed = source[pl.ds(chunk * 256, 256), :]
        apart = jnp.dot(index, mixed, preferred_element_type=jnp.float32).astype(target.dtype)
        for trial in range(TRIALS_HERE):
            target[trial, pl.ds(chunk * 128, 128), :] = apart[trial * 128 : trial * 128 + 128]


def fused(
    shards,
    spikes_hbm,
    pre_one_hbm,
    pre_two_hbm,
    upstream_hbm,
    kernel_one_hbm,
    kernel_two_hbm,
    ids_in,
    out_ref,
    kernels,
    pre_one_in,
    pre_two_in,
    upstream_in,
    spikes_mixed,
    spikes,
    pre_one,
    pre_two,
    grad,
    slope_one,
    taps,
    own,
    wide,
    outgoing,
    diag_in,
    side_in,
    parts,
    arrived,
    ids_mine,
    ids_all,
    picks,
    total,
    load_sems,
    diag_send,
    diag_recv,
    side_send,
    side_recv,
    part_send,
    part_recv,
    id_send,
    id_recv,
):
    section = lax.axis_index("section")
    me = lax.axis_index("trial")
    along_x = section + 1 - 2 * (section % 2)
    along_y = (section + 2) % 4
    across = (along_x + 2) % 4
    rows = parts.shape[2] // shards
    spacings = (SECOND_DILATION, FIRST_DILATION)
    far_first = sorted(range(1, shards), key=lambda step: abs(2 * step - shards))

    loads = [
        pltpu.make_async_copy(source, target, load_sems.at[place])
        for place, (source, target) in enumerate(
            (
                (pre_two_hbm.reshape(pre_two_in.shape), pre_two_in),
                (upstream_hbm.reshape(upstream_in.shape), upstream_in),
                (kernel_two_hbm, kernels.at[0]),
                (pre_one_hbm.reshape(pre_one_in.shape), pre_one_in),
                (kernel_one_hbm, kernels.at[1]),
                (spikes_hbm.reshape(spikes_mixed.shape), spikes_mixed),
            )
        )
    ]
    for load in loads:
        load.start()

    barrier = pltpu.get_barrier_semaphore()
    for partner in (along_x, along_y):
        pl.semaphore_signal(barrier, inc=1, device_id=(partner, me), device_id_type=MESH)
    for step in range(1, shards):
        peer = (me + step) % shards
        pl.semaphore_signal(barrier, inc=1, device_id=(section, peer), device_id_type=MESH)

    row = lax.broadcasted_iota(jnp.int32, (256, 256), 0)
    column = lax.broadcasted_iota(jnp.int32, (256, 256), 1)
    wanted = jnp.where(row < 128, 2 * row, 2 * row - 255)
    index = (column == wanted).astype(jnp.float32).astype(jnp.bfloat16)

    def diag_copy(unit, way, piece):
        partner = (along_x, along_y)[way]
        return pltpu.make_async_remote_copy(
            src_ref=outgoing.at[unit, 2, pl.ds(128 * piece + 64 * way, 64)],
            dst_ref=diag_in.at[unit, way, piece],
            send_sem=diag_send.at[unit, way, piece],
            recv_sem=diag_recv.at[unit, way, piece],
            device_id=(partner, me),
            device_id_type=MESH,
        )

    def side_copy(unit, way, piece, half):
        partner = (along_x, along_y)[way]
        lines = pl.ds(128 * piece + 64 * half, 64)
        return pltpu.make_async_remote_copy(
            src_ref=outgoing.at[unit, way, lines],
            dst_ref=side_in.at[unit, way, lines],
            send_sem=side_send.at[unit, way, piece, half],
            recv_sem=side_recv.at[unit, way, piece, half],
            device_id=(partner, me),
            device_id_type=MESH,
        )

    def flow(layer, lines, upstream, slope):
        rounded = (upstream * slope).astype(jnp.bfloat16).astype(jnp.float32)
        for tap in range(3):
            taps[tap, lines] = shifted(rounded, tap * spacings[layer]).astype(jnp.bfloat16)

    def product(layer, target):
        result = None
        for tap in range(3):
            weights = kernels[layer, tap, pl.ds(pl.multiple_of(target * 256, 256), 256), :]
            term = jnp.dot(weights, taps[tap], preferred_element_type=jnp.float32)
            result = term if result is None else result + term
        return result

    def compute(layer, unit):
        outgoing[unit, 2] = product(layer, across).astype(jnp.bfloat16)
        for piece in range(2):
            for way in range(2):
                diag_copy(unit, way, piece).start()
        for way, partner in enumerate((along_x, along_y)):
            result = product(layer, partner)
            for piece in range(2):
                near, far = 128 * piece + 64 * way, 128 * piece + 64 * (1 - way)
                outgoing[unit, way, pl.ds(near, 64)] = result[near : near + 64].astype(jnp.bfloat16)
                wide[unit, 1 - way, piece] = result[far : far + 64]
                side_copy(unit, way, piece, way).start()
        own[unit] = product(layer, section)

    def forward(unit, piece):
        for way in range(2):
            diag_copy(unit, way, piece).wait_recv()
            joined = wide[unit, way, piece] + diag_in[unit, way, piece].astype(jnp.float32)
            lines = pl.ds(128 * piece + 64 * way, 64)
            outgoing[unit, 1 - way, lines] = joined.astype(jnp.bfloat16)
            side_copy(unit, 1 - way, piece, way).start()

    def finish(unit, trial, piece):
        for way in range(2):
            for half in range(2):
                side_copy(unit, way, piece, half).wait_recv()
        lines = pl.ds(128 * piece, 128)
        first, second = side_in[unit, 0, lines], side_in[unit, 1, lines]
        back = own[unit, lines] + first.astype(jnp.float32) + second.astype(jnp.float32)
        rounded = (grad[trial, lines].astype(jnp.float32) + back).astype(jnp.bfloat16)
        grad[trial, lines] = rounded
        return rounded

    def turn(unit, trial):
        for piece in range(2):
            lines = pl.ds(128 * piece, 128)
            upstream = finish(unit, trial, piece).astype(jnp.float32)
            flow(1, lines, upstream, slope_one[trial, lines])

    def part_copy(trial, piece, step):
        peer = (me + step) % shards
        return pltpu.make_async_remote_copy(
            src_ref=parts.at[trial, piece, pl.ds(pl.multiple_of(peer * rows, rows), rows)],
            dst_ref=arrived.at[trial, piece, pl.ds(pl.multiple_of(me * rows, rows), rows)],
            send_sem=part_send.at[trial, piece, step],
            recv_sem=part_recv.at[trial, piece, step],
            device_id=(section, peer),
            device_id_type=MESH,
        )

    def id_copy(step):
        peer = (me + step) % shards
        return pltpu.make_async_remote_copy(
            src_ref=ids_mine,
            dst_ref=ids_all.at[me],
            send_sem=id_send.at[step],
            recv_sem=id_recv.at[step],
            device_id=(section, peer),
            device_id_type=MESH,
        )

    def readin(trial, piece, gradient):
        both = lax.dot_general(
            spikes[trial], gradient, (((1,), (1,)), ((), ())), preferred_element_type=jnp.float32
        )
        parts[trial, piece] = both.astype(jnp.bfloat16)
        for step in far_first:
            part_copy(trial, piece, step).start()
        mine = pl.ds(pl.multiple_of(me * rows, rows), rows)
        arrived[trial, piece, mine] = parts[trial, piece, mine]

    def collect(trial, piece):
        for step in range(1, shards):
            part_copy(trial, piece, step).wait_recv()
        return jnp.dot(picks[trial], arrived[trial, piece], preferred_element_type=jnp.float32)

    whole = pl.ds(0, 256)
    loads[0].wait()
    split_pairs(pre_two_in, index, pre_two, 2)
    loads[1].wait()
    split_pairs(upstream_in, index, grad, 2)
    flow(0, whole, grad[0].astype(jnp.float32), gelu_slope(pre_two[0]))
    loads[2].wait()
    pl.semaphore_wait(barrier, shards + 1)
    compute(0, 0)

    flow(0, whole, grad[1].astype(jnp.float32), gelu_slope(pre_two[1]))
    forward(0, 0)
    forward(0, 1)
    compute(0, 1)

    top = lax.broadcasted_iota(jnp.int32, ids_mine.shape, 0)
    ids_mine[...] = jnp.where(top == 0, ids_in[0], ids_in[1])
    for step in range(1, shards):
        id_copy(step).start()
    ids_all[me] = ids_mine[...]

    loads[3].wait()
    split_pairs(pre_one_in, index, pre_one, 2)
    for trial in range(TRIALS_HERE):
        slope_one[trial] = gelu_slope(pre_one[trial])
    forward(1, 0)
    forward(1, 1)

    loads[4].wait()
    turn(0, 0)
    compute(1, 2)

    turn(1, 1)
    forward(2, 0)
    forward(2, 1)
    compute(1, 3)

    loads[5].wait()
    split_pairs(spikes_mixed, index, spikes, spikes_mixed.shape[0] // 256)

    readin(0, 0, finish(2, 0, 0))
    forward(3, 0)
    forward(3, 1)
    readin(0, 1, finish(2, 0, 1))

    for step in range(1, shards):
        id_copy(step).wait_recv()
    line = lax.broadcasted_iota(jnp.int32, (shards * rows, 128), 0)
    lane = lax.broadcasted_iota(jnp.int32, (shards * rows, 128), 1)
    same = (line % rows) == (lane % rows)
    session = line // rows
    per = 128 // rows
    for trial in range(TRIALS_HERE):
        for piece in range(shards * rows // 128):
            known = ids_all[piece * per, pl.ds(trial, 1), :]
            for slot in range(1, per):
                other = ids_all[piece * per + slot, pl.ds(trial, 1), :]
                known = jnp.where(lane[:1] < slot * rows, known, other)
            chosen = same & (session == known)
            picks[trial, :, pl.ds(piece * 128, 128)] = chosen.astype(jnp.float32).astype(jnp.bfloat16)

    for piece in range(2):
        readin(1, piece, finish(3, 1, piece))
    for piece in range(2):
        total[piece] = collect(0, piece)
    for piece in range(2):
        summed = (total[piece] + collect(1, piece)).astype(jnp.bfloat16)
        out_ref[:, :, pl.ds(128 * piece, 128)] = summed.reshape(shards, rows, 128)

    for piece in range(2):
        for unit in range(4):
            for way in range(2):
                diag_copy(unit, way, piece).wait_send()
                for half in range(2):
                    side_copy(unit, way, piece, half).wait_send()
        for step in range(1, shards):
            for trial in range(TRIALS_HERE):
                part_copy(trial, piece, step).wait_send()
    for step in range(1, shards):
        id_copy(step).wait_send()


def one_kernel(
    spike_rates,
    first_preactivation,
    second_preactivation,
    output_gradient,
    first_kernel,
    second_kernel,
    session_of,
):
    shards = lax.axis_size("trial")
    neurons, trials, steps = spike_rates.shape
    block = output_gradient.shape[0]
    rows = neurons // shards
    f32, bf16 = jnp.float32, jnp.bfloat16
    vmem = pl.BlockSpec(memory_space=pltpu.VMEM)
    hbm = pl.BlockSpec(memory_space=pltpu.HBM)
    dma = pltpu.SemaphoreType.DMA

    return pl.pallas_call(
        functools.partial(fused, shards),
        out_shape=jax.ShapeDtypeStruct((shards, rows, block), bf16),
        in_specs=[
            hbm,
            hbm,
            hbm,
            hbm,
            hbm,
            hbm,
            pl.BlockSpec(memory_space=pltpu.SMEM),
        ],
        out_specs=vmem,
        scratch_shapes=[
            pltpu.VMEM((2,) + first_kernel.shape, bf16),
            pltpu.VMEM((block * trials, steps), bf16),
            pltpu.VMEM((block * trials, steps), bf16),
            pltpu.VMEM((block * trials, steps), bf16),
            pltpu.VMEM((neurons * trials, steps), bf16),
            pltpu.VMEM((trials, neurons, steps), bf16),
            pltpu.VMEM((trials, block, steps), bf16),
            pltpu.VMEM((trials, block, steps), bf16),
            pltpu.VMEM((trials, block, steps), bf16),
            pltpu.VMEM((trials, block, steps), f32),
            pltpu.VMEM((3, block, steps), bf16),
            pltpu.VMEM((4, block, steps), f32),
            pltpu.VMEM((4, 2, 2, block // 4, steps), f32),
            pltpu.VMEM((4, 3, block, steps), bf16),
            pltpu.VMEM((4, 2, 2, block // 4, steps), bf16),
            pltpu.VMEM((4, 2, block, steps), bf16),
            pltpu.VMEM((trials, 2, neurons, block // 2), bf16),
            pltpu.VMEM((trials, 2, neurons, block // 2), bf16),
            pltpu.VMEM((8, 128), jnp.int32),
            pltpu.VMEM((shards, 8, 128), jnp.int32),
            pltpu.VMEM((trials, shards * rows, shards * rows), bf16),
            pltpu.VMEM((2, shards * rows, block // 2), f32),
            dma((6,)),
            dma((4, 2, 2)),
            dma((4, 2, 2)),
            dma((4, 2, 2, 2)),
            dma((4, 2, 2, 2)),
            dma((trials, 2, shards)),
            dma((trials, 2, shards)),
            dma((shards,)),
            dma((shards,)),
        ],
        compiler_params=pltpu.CompilerParams(
            collective_id=0, has_side_effects=True, vmem_limit_bytes=63 * 1024 * 1024
        ),
        cost_estimate=pl.CostEstimate(
            flops=2_000_000_000, bytes_accessed=6_000_000, transcendentals=500_000
        ),
    )(
        spike_rates,
        first_preactivation,
        second_preactivation,
        output_gradient,
        first_kernel,
        second_kernel,
        session_of,
    )


def choose(mesh, spike_rates, *others):
    shards = mesh.shape["trial"]
    neurons, trials, steps = spike_rates.shape
    rows = neurons // shards
    fits = mesh.shape["section"] == 4 and trials == TRIALS_HERE and steps == 256
    fits = fits and others[0].shape[0] == 256 and neurons % 128 == 0 and rows in (16, 32, 64, 128)
    return (one_kernel if fits else body)(spike_rates, *others)


def solution(mesh):
    in_specs = (
        P(None, "trial", None),
        P("section", "trial", None),
        P("section", "trial", None),
        P("section", "trial", None),
        P(None, None, "section"),
        P(None, None, "section"),
        P("trial"),
    )
    out_specs = P(None, "trial", "section")
    run = functools.partial(choose, mesh)
    return jax.shard_map(run, mesh=mesh, in_specs=in_specs, out_specs=out_specs, check_vma=False)
```

```python
import functools
import math

import jax
import jax.numpy as jnp
from jax import lax
from jax.experimental import pallas as pl
from jax.experimental.pallas import tpu as pltpu
from jax.sharding import PartitionSpec as P

FIRST_DILATION = 32
SECOND_DILATION = 64
MOST = 6


def gelu_slope(preact):
    values = preact.astype(jnp.float32)
    normal_cdf = 0.5 * (1.0 + lax.erf(values * (1.0 / math.sqrt(2.0))))
    density = jnp.exp(-0.5 * values * values) * (1.0 / math.sqrt(2.0 * math.pi))
    return normal_cdf + values * density


def shift_ahead(values, offset):
    padding = [(0, 0)] * (values.ndim - 1) + [(0, offset)]
    return jnp.pad(values[..., offset:], padding)


def tap_sum(weights, flow_grad, spacing):
    running = None
    for kernel_tap in range(3):
        term_tap = lax.dot_general(
            weights[kernel_tap],
            flow_grad,
            (((1,), (0,)), ((), ())),
            preferred_element_type=jnp.float32,
        )
        if kernel_tap > 0:
            term_tap = shift_ahead(term_tap, kernel_tap * spacing)
        running = term_tap if running is None else running + term_tap
    return running


def layer_backprop(upstream, preact, turned, spacing):
    flow_grad = (upstream.astype(jnp.float32) * gelu_slope(preact)).astype(jnp.bfloat16)
    back_sum = tap_sum(turned, lax.all_gather(flow_grad, "section", axis=0, tiled=True), spacing)
    return (upstream.astype(jnp.float32) + back_sum).astype(jnp.bfloat16)


def body(
    spike_rates,
    first_preactivation,
    second_preactivation,
    output_gradient,
    first_kernel,
    second_kernel,
    session_of,
):
    first_flipped_kernel, second_flipped_kernel = (
        lax.all_to_all(first_kernel, "section", split_axis=1, concat_axis=2, tiled=True),
        lax.all_to_all(second_kernel, "section", split_axis=1, concat_axis=2, tiled=True),
    )
    upstream_gradient = layer_backprop(
        output_gradient, second_preactivation, second_flipped_kernel, SECOND_DILATION
    )
    input_gradient = layer_backprop(
        upstream_gradient, first_preactivation, first_flipped_kernel, FIRST_DILATION
    )
    trial_shards = lax.axis_size("trial")
    neurons, trials, steps_count = spike_rates.shape
    neuron_blocks = spike_rates.reshape(trial_shards, neurons // trial_shards, trials, steps_count)
    partials = jnp.einsum(
        "jbil,cil->jibc", neuron_blocks, input_gradient, preferred_element_type=jnp.float32
    )
    arrived = lax.all_to_all(
        partials.astype(jnp.bfloat16), "trial", split_axis=0, concat_axis=0, tiled=True
    ).astype(partials.dtype)
    every_id = lax.all_gather(session_of, "trial", axis=0, tiled=True)
    total_trials = every_id.shape[0]
    flat_parts = arrived.reshape(total_trials, -1)
    session_list = jnp.arange(trial_shards, dtype=jnp.int32)
    first_trial = jnp.sum((every_id[None, :] < session_list[:, None]).astype(jnp.int32), axis=1)

    def add_offset(offset, running):
        position = first_trial + offset
        clipped = jnp.minimum(position, total_trials - 1)
        rows_here = jnp.take(flat_parts, clipped, axis=0)
        valid = (position < total_trials) & (jnp.take(every_id, clipped, axis=0) == session_list)
        return running + jnp.where(valid[:, None], rows_here, 0.0)

    start_sums = jnp.zeros((trial_shards, flat_parts.shape[1]), jnp.float32)
    summed = lax.fori_loop(0, MOST, add_offset, start_sums)
    return summed.reshape(trial_shards, neurons // trial_shards, input_gradient.shape[0]).astype(
        jnp.bfloat16
    )


MESH = pl.DeviceIdType.MESH
TRIALS_HERE = 2


def shifted(values, offset):
    if offset == 0:
        return values
    width = values.shape[1]
    rolled = pltpu.roll(values, width - offset, 1)
    lane = lax.broadcasted_iota(jnp.int32, values.shape, 1)
    return jnp.where(lane < width - offset, rolled, 0.0)


def split_pairs(source, index, target, halves):
    for chunk in range(halves):
        mixed = source[pl.ds(chunk * 256, 256), :]
        apart = jnp.dot(index, mixed, preferred_element_type=jnp.float32).astype(target.dtype)
        for trial in range(TRIALS_HERE):
            target[trial, pl.ds(chunk * 128, 128), :] = apart[trial * 128 : trial * 128 + 128]


def fused(
    shards,
    spikes_hbm,
    pre_one_hbm,
    pre_two_hbm,
    upstream_hbm,
    kernel_one_hbm,
    kernel_two_hbm,
    ids_in,
    out_ref,
    kernels,
    pre_one_in,
    pre_two_in,
    upstream_in,
    spikes_mixed,
    spikes,
    pre_one,
    pre_two,
    grad,
    slope_one,
    taps,
    own,
    wide,
    outgoing,
    diag_in,
    side_in,
    parts,
    arrived,
    ids_mine,
    ids_all,
    picks,
    total,
    load_sems,
    diag_send,
    diag_recv,
    side_send,
    side_recv,
    part_send,
    part_recv,
    id_send,
    id_recv,
):
    section = lax.axis_index("section")
    me = lax.axis_index("trial")
    along_x = section + 1 - 2 * (section % 2)
    along_y = (section + 2) % 4
    across = (along_x + 2) % 4
    rows = parts.shape[2] // shards
    spacings = (SECOND_DILATION, FIRST_DILATION)
    far_first = sorted(range(1, shards), key=lambda step: abs(2 * step - shards))

    loads = [
        pltpu.make_async_copy(source, target, load_sems.at[place])
        for place, (source, target) in enumerate(
            (
                (pre_two_hbm.reshape(pre_two_in.shape), pre_two_in),
                (upstream_hbm.reshape(upstream_in.shape), upstream_in),
                (kernel_two_hbm, kernels.at[0]),
                (pre_one_hbm.reshape(pre_one_in.shape), pre_one_in),
                (kernel_one_hbm, kernels.at[1]),
                (spikes_hbm.reshape(spikes_mixed.shape), spikes_mixed),
            )
        )
    ]
    for load in loads:
        load.start()

    barrier = pltpu.get_barrier_semaphore()
    for partner in (along_x, along_y):
        pl.semaphore_signal(barrier, inc=1, device_id=(partner, me), device_id_type=MESH)
    for step in range(1, shards):
        peer = (me + step) % shards
        pl.semaphore_signal(barrier, inc=1, device_id=(section, peer), device_id_type=MESH)

    row = lax.broadcasted_iota(jnp.int32, (256, 256), 0)
    column = lax.broadcasted_iota(jnp.int32, (256, 256), 1)
    wanted = jnp.where(row < 128, 2 * row, 2 * row - 255)
    index = (column == wanted).astype(jnp.float32).astype(jnp.bfloat16)

    def diag_copy(unit, way, piece):
        partner = (along_x, along_y)[way]
        return pltpu.make_async_remote_copy(
            src_ref=outgoing.at[unit, 2, pl.ds(128 * piece + 64 * way, 64)],
            dst_ref=diag_in.at[unit, way, piece],
            send_sem=diag_send.at[unit, way, piece],
            recv_sem=diag_recv.at[unit, way, piece],
            device_id=(partner, me),
            device_id_type=MESH,
        )

    def side_copy(unit, way, piece, half):
        partner = (along_x, along_y)[way]
        lines = pl.ds(128 * piece + 64 * half, 64)
        return pltpu.make_async_remote_copy(
            src_ref=outgoing.at[unit, way, lines],
            dst_ref=side_in.at[unit, way, lines],
            send_sem=side_send.at[unit, way, piece, half],
            recv_sem=side_recv.at[unit, way, piece, half],
            device_id=(partner, me),
            device_id_type=MESH,
        )

    def flow(layer, lines, upstream, slope):
        rounded = (upstream * slope).astype(jnp.bfloat16).astype(jnp.float32)
        for tap in range(3):
            taps[tap, lines] = shifted(rounded, tap * spacings[layer]).astype(jnp.bfloat16)

    def product(layer, target):
        result = None
        for tap in range(3):
            weights = kernels[layer, tap, pl.ds(pl.multiple_of(target * 256, 256), 256), :]
            term = jnp.dot(weights, taps[tap], preferred_element_type=jnp.float32)
            result = term if result is None else result + term
        return result

    def compute(layer, unit):
        outgoing[unit, 2] = product(layer, across).astype(jnp.bfloat16)
        for piece in range(2):
            for way in range(2):
                diag_copy(unit, way, piece).start()
        for way, partner in enumerate((along_x, along_y)):
            result = product(layer, partner)
            for piece in range(2):
                near, far = 128 * piece + 64 * way, 128 * piece + 64 * (1 - way)
                outgoing[unit, way, pl.ds(near, 64)] = result[near : near + 64].astype(jnp.bfloat16)
                wide[unit, 1 - way, piece] = result[far : far + 64]
                side_copy(unit, way, piece, way).start()
        own[unit] = product(layer, section)

    def forward(unit, piece):
        for way in range(2):
            diag_copy(unit, way, piece).wait_recv()
            joined = wide[unit, way, piece] + diag_in[unit, way, piece].astype(jnp.float32)
            lines = pl.ds(128 * piece + 64 * way, 64)
            outgoing[unit, 1 - way, lines] = joined.astype(jnp.bfloat16)
            side_copy(unit, 1 - way, piece, way).start()

    def finish(unit, trial, piece):
        for way in range(2):
            for half in range(2):
                side_copy(unit, way, piece, half).wait_recv()
        lines = pl.ds(128 * piece, 128)
        first, second = side_in[unit, 0, lines], side_in[unit, 1, lines]
        back = own[unit, lines] + first.astype(jnp.float32) + second.astype(jnp.float32)
        rounded = (grad[trial, lines].astype(jnp.float32) + back).astype(jnp.bfloat16)
        grad[trial, lines] = rounded
        return rounded

    def turn(unit, trial):
        for piece in range(2):
            lines = pl.ds(128 * piece, 128)
            upstream = finish(unit, trial, piece).astype(jnp.float32)
            flow(1, lines, upstream, slope_one[trial, lines])

    def part_copy(trial, piece, step):
        peer = (me + step) % shards
        return pltpu.make_async_remote_copy(
            src_ref=parts.at[trial, piece, pl.ds(pl.multiple_of(peer * rows, rows), rows)],
            dst_ref=arrived.at[trial, piece, pl.ds(pl.multiple_of(me * rows, rows), rows)],
            send_sem=part_send.at[trial, piece, step],
            recv_sem=part_recv.at[trial, piece, step],
            device_id=(section, peer),
            device_id_type=MESH,
        )

    def id_copy(step):
        peer = (me + step) % shards
        return pltpu.make_async_remote_copy(
            src_ref=ids_mine,
            dst_ref=ids_all.at[me],
            send_sem=id_send.at[step],
            recv_sem=id_recv.at[step],
            device_id=(section, peer),
            device_id_type=MESH,
        )

    def readin(trial, piece, gradient):
        both = lax.dot_general(
            spikes[trial], gradient, (((1,), (1,)), ((), ())), preferred_element_type=jnp.float32
        )
        parts[trial, piece] = both.astype(jnp.bfloat16)
        for step in far_first:
            part_copy(trial, piece, step).start()
        mine = pl.ds(pl.multiple_of(me * rows, rows), rows)
        arrived[trial, piece, mine] = parts[trial, piece, mine]

    def collect(trial, piece):
        for step in range(1, shards):
            part_copy(trial, piece, step).wait_recv()
        return jnp.dot(picks[trial], arrived[trial, piece], preferred_element_type=jnp.float32)

    whole = pl.ds(0, 256)
    loads[0].wait()
    split_pairs(pre_two_in, index, pre_two, 2)
    loads[1].wait()
    split_pairs(upstream_in, index, grad, 2)
    flow(0, whole, grad[0].astype(jnp.float32), gelu_slope(pre_two[0]))
    loads[2].wait()
    pl.semaphore_wait(barrier, shards + 1)
    compute(0, 0)

    flow(0, whole, grad[1].astype(jnp.float32), gelu_slope(pre_two[1]))
    forward(0, 0)
    forward(0, 1)
    compute(0, 1)

    top = lax.broadcasted_iota(jnp.int32, ids_mine.shape, 0)
    ids_mine[...] = jnp.where(top == 0, ids_in[0], ids_in[1])
    for step in range(1, shards):
        id_copy(step).start()
    ids_all[me] = ids_mine[...]

    loads[3].wait()
    split_pairs(pre_one_in, index, pre_one, 2)
    slope_one[0] = gelu_slope(pre_one[0])
    forward(1, 0)
    forward(1, 1)

    loads[4].wait()
    turn(0, 0)
    compute(1, 2)

    slope_one[1] = gelu_slope(pre_one[1])
    turn(1, 1)
    forward(2, 0)
    forward(2, 1)
    compute(1, 3)

    loads[5].wait()
    split_pairs(spikes_mixed, index, spikes, spikes_mixed.shape[0] // 256)

    readin(0, 0, finish(2, 0, 0))
    forward(3, 0)
    forward(3, 1)
    readin(0, 1, finish(2, 0, 1))

    for step in range(1, shards):
        id_copy(step).wait_recv()
    line = lax.broadcasted_iota(jnp.int32, (shards * rows, 128), 0)
    lane = lax.broadcasted_iota(jnp.int32, (shards * rows, 128), 1)
    same = (line % rows) == (lane % rows)
    session = line // rows
    per = 128 // rows
    for trial in range(TRIALS_HERE):
        for piece in range(shards * rows // 128):
            known = ids_all[piece * per, pl.ds(trial, 1), :]
            for slot in range(1, per):
                other = ids_all[piece * per + slot, pl.ds(trial, 1), :]
                known = jnp.where(lane[:1] < slot * rows, known, other)
            chosen = same & (session == known)
            picks[trial, :, pl.ds(piece * 128, 128)] = chosen.astype(jnp.float32).astype(jnp.bfloat16)

    for piece in range(2):
        readin(1, piece, finish(3, 1, piece))
    for piece in range(2):
        total[piece] = collect(0, piece)
    for piece in range(2):
        summed = (total[piece] + collect(1, piece)).astype(jnp.bfloat16)
        out_ref[:, :, pl.ds(128 * piece, 128)] = summed.reshape(shards, rows, 128)

    for piece in range(2):
        for unit in range(4):
            for way in range(2):
                diag_copy(unit, way, piece).wait_send()
                for half in range(2):
                    side_copy(unit, way, piece, half).wait_send()
        for step in range(1, shards):
            for trial in range(TRIALS_HERE):
                part_copy(trial, piece, step).wait_send()
    for step in range(1, shards):
        id_copy(step).wait_send()


def one_kernel(
    spike_rates,
    first_preactivation,
    second_preactivation,
    output_gradient,
    first_kernel,
    second_kernel,
    session_of,
):
    shards = lax.axis_size("trial")
    neurons, trials, steps = spike_rates.shape
    block = output_gradient.shape[0]
    rows = neurons // shards
    f32, bf16 = jnp.float32, jnp.bfloat16
    vmem = pl.BlockSpec(memory_space=pltpu.VMEM)
    hbm = pl.BlockSpec(memory_space=pltpu.HBM)
    dma = pltpu.SemaphoreType.DMA

    return pl.pallas_call(
        functools.partial(fused, shards),
        out_shape=pltpu.VMEM((shards, rows, block), bf16),
        in_specs=[
            hbm,
            hbm,
            hbm,
            hbm,
            hbm,
            hbm,
            pl.BlockSpec(memory_space=pltpu.SMEM),
        ],
        out_specs=vmem,
        scratch_shapes=[
            pltpu.VMEM((2,) + first_kernel.shape, bf16),
            pltpu.VMEM((block * trials, steps), bf16),
            pltpu.VMEM((block * trials, steps), bf16),
            pltpu.VMEM((block * trials, steps), bf16),
            pltpu.VMEM((neurons * trials, steps), bf16),
            pltpu.VMEM((trials, neurons, steps), bf16),
            pltpu.VMEM((trials, block, steps), bf16),
            pltpu.VMEM((trials, block, steps), bf16),
            pltpu.VMEM((trials, block, steps), bf16),
            pltpu.VMEM((trials, block, steps), f32),
            pltpu.VMEM((3, block, steps), bf16),
            pltpu.VMEM((4, block, steps), f32),
            pltpu.VMEM((4, 2, 2, block // 4, steps), f32),
            pltpu.VMEM((4, 3, block, steps), bf16),
            pltpu.VMEM((4, 2, 2, block // 4, steps), bf16),
            pltpu.VMEM((4, 2, block, steps), bf16),
            pltpu.VMEM((trials, 2, neurons, block // 2), bf16),
            pltpu.VMEM((trials, 2, neurons, block // 2), bf16),
            pltpu.VMEM((8, 128), jnp.int32),
            pltpu.VMEM((shards, 8, 128), jnp.int32),
            pltpu.VMEM((trials, shards * rows, shards * rows), bf16),
            pltpu.VMEM((2, shards * rows, block // 2), f32),
            dma((6,)),
            dma((4, 2, 2)),
            dma((4, 2, 2)),
            dma((4, 2, 2, 2)),
            dma((4, 2, 2, 2)),
            dma((trials, 2, shards)),
            dma((trials, 2, shards)),
            dma((shards,)),
            dma((shards,)),
        ],
        compiler_params=pltpu.CompilerParams(
            collective_id=0, has_side_effects=True, vmem_limit_bytes=60 * 1024 * 1024
        ),
        cost_estimate=pl.CostEstimate(
            flops=2_000_000_000, bytes_accessed=6_000_000, transcendentals=500_000
        ),
    )(
        spike_rates,
        first_preactivation,
        second_preactivation,
        output_gradient,
        first_kernel,
        second_kernel,
        session_of,
    )


def choose(mesh, spike_rates, *others):
    shards = mesh.shape["trial"]
    neurons, trials, steps = spike_rates.shape
    rows = neurons // shards
    fits = mesh.shape["section"] == 4 and trials == TRIALS_HERE and steps == 256
    fits = fits and others[0].shape[0] == 256 and neurons % 128 == 0 and rows in (16, 32, 64, 128)
    return (one_kernel if fits else body)(spike_rates, *others)


def solution(mesh):
    in_specs = (
        P(None, "trial", None),
        P("section", "trial", None),
        P("section", "trial", None),
        P("section", "trial", None),
        P(None, None, "section"),
        P(None, None, "section"),
        P("trial"),
    )
    out_specs = P(None, "trial", "section")
    run = functools.partial(choose, mesh)
    return jax.shard_map(run, mesh=mesh, in_specs=in_specs, out_specs=out_specs, check_vma=False)
```
